256 devices in a mesh: col: 128 (over x, y, z), rep: 2 (over core).
Axes of the slice: x: 4, y: 4, z: 8, core: 2. Of those that a mesh axis runs over, the one named last changes fastest.
Arguments:
- features: bfloat16 [32768, 256], P('col'), may hold values from -6 to 6
- src_norm: bfloat16 [32768], P('col'), may hold values from 0.049804688 to 1
- dst_norm: float32 [524288], P('col'), may hold values from 0.05 to 1
- src_block: int32 [128, 2, 128], P('col', 'rep'), may hold values from 0 to 255, as said below
- dst_block: int32 [128, 2, 128], P('col', 'rep'), may hold values from 0 to 31
- counts: int32 [128, 2, 128, 128, 128], P('col', 'rep'), may hold values from 0 to 3, as said below
- weight: bfloat16 [256, 256], replicated, may hold values from -0.375 to 0.375
- out_bias: bfloat16 [256], replicated, may hold values from -3 to 3
Outputs:
- activated: bfloat16 [524288, 256], P(('col', 'rep'))
The draws below stay inside these ranges and needn't reach their ends.
Inputs may be any that keep to these rules, and one draw needn't show every extreme that they name: For each (c, r) and each index p of col, the entries src_block[c, r, :] that lie in [p * 2, (p + 1) * 2) are all equal: a device's blocks name at most one source block of each index of col. `counts`: most entries are zero.
All inputs are finite; a program needn't handle non-finite values.
Results may differ from the reference program's by a relative error of at most 0.0055.
Values may be sent and summed in bfloat16 or wider, within the bound.
No kernel may reach another device: no remote copies, remote signals or barrier semaphores. Data moves between devices by JAX's collectives and lax.ppermute only.
A program may use at most 128 MiB of HBM per device.

```python
import math
import jax
import jax.numpy as jnp
import numpy as np
from jax import lax

F = 256
BLOCK = 128
DST_BLK = 32
SRC_BLK = 2
NB = 128
NDST = 524288
NSRC = 32768
N_COL = 128
N_REP = 2


def draw_src_block(key, part):
    key = jax.random.fold_in(key, 11)
    key_pick, key_holder = jax.random.split(key)
    picked = jax.random.randint(key_pick, (N_COL, N_REP, N_COL), 0, SRC_BLK)
    holder = jax.random.randint(key_holder, (N_COL, N_REP, NB), 0, N_COL)
    local_pick = jnp.take_along_axis(picked, holder, axis=2)
    return (holder * SRC_BLK + local_pick).astype(jnp.int32)


def draw_counts(key, part):
    key = jax.random.fold_in(key, 23)
    key_live, key_mult = jax.random.split(key)
    shape = (N_COL, N_REP, NB, BLOCK, BLOCK)
    live = jax.random.randint(key_live, shape, 0, BLOCK) < 4
    multiple = jax.random.randint(key_mult, shape, 1, 4)
    return jnp.where(live, multiple, 0).astype(jnp.int32)


def touch_ends(drawn, key, low, high):
    longest = drawn.shape.index(max(drawn.shape))
    spots = []
    for shift in (0, 1):
        where = [jax.random.randint(jax.random.fold_in(key, axis), (), 0, length) for axis, length in enumerate(drawn.shape)]
        where[longest] = (where[longest] + shift) % drawn.shape[longest]
        spots.append(tuple(where))
    return drawn.at[spots[0]].set(low).at[spots[1]].set(high)


def level_of(own_key, dims, pieces, low, top_value):
    factor_of, own = 1.0, jax.random.fold_in(own_key, 6)
    for position, shards_of in pieces:
        heights = jnp.exp(jax.random.uniform(jax.random.fold_in(own, position), (shards_of,), jnp.float32, low / len(pieces), top_value / len(pieces)))
        factor_of = factor_of * jnp.repeat(heights, dims[position] // shards_of).reshape([-1 if axis == position else 1 for axis in range(len(dims))])
    return factor_of


def rank_table(count, lean):
    loads = [(1 << 20) // math.isqrt(standing ** lean) + 1 for standing in range(1, count + 1)]
    spread = 1 + sum(loads) // (1 << 30)
    return np.cumsum(np.array([max(1, weight // spread) for weight in loads]))


def skewed_ids(own_key, extent, number_of, lean):
    table = rank_table(number_of, lean)
    pick = jax.random.randint(jax.random.fold_in(own_key, 1), extent, 0, int(table[number_of - 1]))
    grade = jnp.searchsorted(jnp.asarray(table, jnp.int32), pick, side="right")
    return jax.random.permutation(jax.random.fold_in(own_key, 2), number_of)[grade].astype(jnp.int32)


def normal_values(rng, extent, deviation, most, pieces=(), held_as=jnp.bfloat16):
    values = deviation * jax.random.normal(rng, extent, jnp.float32)
    if pieces:
        values = values * level_of(rng, extent, pieces, -0.22, 0.18)
    return jnp.clip(values, -most, most).astype(held_as)


def setup_inputs(seed: int = 0) -> dict:
    streams_of = jax.random.split(jax.random.key(seed), 9)
    features = normal_values(streams_of[0], (NSRC, F), 1.0, 6.0, ((0, 128),))
    src_norm = jnp.clip(jnp.exp(math.log(1.0) - 2.9996462 * jax.random.uniform(streams_of[1], (NSRC,), jnp.float32) ** level_of(streams_of[1], (NSRC,), ((0, 128),), -0.2, 0.2)), 0.049804688, 1.0).astype(jnp.bfloat16)
    dst_norm = jnp.clip(jnp.exp(math.log(1.0) - 2.9957323 * jax.random.uniform(streams_of[2], (NDST,), jnp.float32) ** level_of(streams_of[2], (NDST,), ((0, 128),), -0.2, 0.2)), 0.05, 1.0)
    src_block = draw_src_block(jax.random.fold_in(streams_of[8], 71), 0)
    dst_block = touch_ends(skewed_ids(streams_of[4], (N_COL, N_REP, NB), DST_BLK, 2), jax.random.fold_in(streams_of[4], 3), 0, DST_BLK - 1).astype(jnp.int32)
    counts = draw_counts(jax.random.fold_in(streams_of[8], 71), 0)
    weight = normal_values(streams_of[6], (F, F), F ** -0.5, 0.375)
    out_bias = normal_values(streams_of[7], (F,), 0.5, 3.0)
    return {"features": features, "src_norm": src_norm, "dst_norm": dst_norm, "src_block": src_block, "dst_block": dst_block, "counts": counts, "weight": weight, "out_bias": out_bias}


def reference(features, src_norm, dst_norm, src_block, dst_block, counts, weight, out_bias):
    feat_blocks = features.reshape(-1, BLOCK, F)
    norm_blocks = src_norm.reshape(-1, BLOCK)

    def per_column(inputs):
        src_ids, dst_ids, count_col = inputs
        src_ids = src_ids.reshape(-1).astype(jnp.int32)
        dst_ids = dst_ids.reshape(-1).astype(jnp.int32)
        gathered = feat_blocks[src_ids]
        norm_vals = norm_blocks[src_ids].astype(jnp.float32)
        tile_vals = (count_col.reshape(-1, BLOCK, BLOCK).astype(jnp.float32) * norm_vals[:, None, :]).astype(jnp.bfloat16)
        products = jnp.einsum("bij,bjf->bif", tile_vals.astype(jnp.float32), gathered.astype(jnp.float32),
                              precision=lax.Precision.HIGHEST)
        summed = jax.ops.segment_sum(products, dst_ids, num_segments=DST_BLK)
        return summed.reshape(DST_BLK * BLOCK, F)

    partial_rows = lax.map(per_column, (src_block, dst_block, counts))
    aggregate = partial_rows.reshape(-1, F) * dst_norm[:, None]
    hidden = aggregate.astype(jnp.bfloat16)
    result = jnp.dot(hidden, weight, preferred_element_type=jnp.float32) + out_bias.astype(jnp.float32)
    return jax.nn.relu(result).astype(jnp.bfloat16)
```

```python
import jax
import jax.numpy as jnp
from jax import lax
from jax.experimental import pallas as pl
from jax.experimental.pallas import tpu as pltpu
from jax.sharding import PartitionSpec as P

BLOCK = 128
DST_BLK = 32
WIDTH = 256
NX, NY, NZ = 4, 4, 8
GROUP = 4
HALF_ROWS = 16 * BLOCK + 16
MAX_GROUPS = 256 // GROUP + DST_BLK
SLOTS = MAX_GROUPS * GROUP
MIB = 1024 * 1024


def device(x, y, z, r):
    return (((x % NX) * NY + (y % NY)) * NZ + (z % NZ)) * 2 + r


def from_z(step):
    return [
        (device(x, y, z + step, r), device(x, y, z, r))
        for x in range(NX) for y in range(NY) for z in range(NZ) for r in range(2)
    ]


def from_second(step):
    return [
        (device(x, y + step, z, 0) if r == 0 else device(x + step, y, z, 1), device(x, y, z, r))
        for x in range(NX) for y in range(NY) for z in range(NZ) for r in range(2)
    ]


def from_third(step):
    return [
        (device(x + step, y, z, 0) if r == 0 else device(x, y + step, z, 1), device(x, y, z, r))
        for x in range(NX) for y in range(NY) for z in range(NZ) for r in range(2)
    ]


def move(value, pairs):
    return lax.ppermute(value, ("col", "rep"), pairs)


def sort_kernel(place, src, dst, start, tiles, blocks, norms, count, cursor):
    z, second, third, rep = place[0], place[1], place[2], place[3]

    def clear(k, carry):
        count[k] = 0
        return carry

    lax.fori_loop(0, DST_BLK, clear, 0)

    def blank(s, carry):
        tiles[s] = 0
        blocks[s] = 0
        norms[s] = 128
        return carry

    lax.fori_loop(0, SLOTS, blank, 0)

    def key_of(e):
        return (dst[e] + 16 * (1 - rep)) & 31

    def tally(e, carry):
        k = key_of(e)
        count[k] = count[k] + jnp.where((src[e] & 1) == rep, 1, 0)
        return carry

    lax.fori_loop(0, 256, tally, 0)

    def offsets(k, at):
        start[k] = at
        cursor[k] = at * GROUP
        return at + ((count[k] + (GROUP - 1)) >> 2)

    start[DST_BLK] = lax.fori_loop(0, DST_BLK, offsets, 0)

    def put(e, carry):
        block = src[e]

        @pl.when((block & 1) == rep)
        def _():
            k = key_of(e)
            s = cursor[k]
            cursor[k] = s + 1
            p = block >> 1
            px, py, pz = p >> 5, (p >> 3) & 3, p & 7
            pa = jnp.where(rep == 0, py, px)
            pb = jnp.where(rep == 0, px, py)
            dz, da, db = (pz - z) & 7, (pa - second) & 3, (pb - third) & 3
            index = db * 32 + da * 8 + dz
            tiles[s] = e
            blocks[s] = index
            norms[s] = index

        return carry

    lax.fori_loop(0, 256, put, 0)


def sort_blocks(place, src, dst):
    smem = pl.BlockSpec(memory_space=pltpu.SMEM)
    slots = jax.ShapeDtypeStruct((SLOTS,), jnp.int32)
    return pl.pallas_call(
        sort_kernel,
        out_shape=(jax.ShapeDtypeStruct((DST_BLK + 1,), jnp.int32), slots, slots, slots),
        in_specs=[smem] * 3,
        out_specs=(smem,) * 4,
        scratch_shapes=[pltpu.SMEM((DST_BLK,), jnp.int32), pltpu.SMEM((DST_BLK,), jnp.int32)],
    )(place, src, dst)


def sum_kernel(start, tiles, blocks, norms, *refs):
    pieces, own_tiles, other_tiles = refs[:8], refs[8], refs[9]
    sent, kept = refs[10], refs[11]
    feat, tile, norm, sems = refs[12:]
    copies = [pltpu.make_async_copy(pieces[i], feat.at[i], sems.at[i]) for i in range(8)]
    copies.append(pltpu.make_async_copy(own_tiles, tile.at[pl.ds(0, 128)], sems.at[8]))
    copies.append(pltpu.make_async_copy(other_tiles, tile.at[pl.ds(128, 128)], sems.at[9]))
    for copy in copies:
        copy.start()
    for copy in copies:
        copy.wait()
    for i in range(8):
        norm[pl.ds(16 * i, 16), :] = feat[i, pl.ds(16 * BLOCK, 16), pl.ds(0, BLOCK)].astype(jnp.float32)
    norm[pl.ds(128, 8), :] = jnp.zeros((8, BLOCK), jnp.float32)

    def add_group(g, total):
        left, right = [], []
        for u in range(GROUP):
            s = g * GROUP + u
            index = blocks[s]
            scale = norm[pl.ds(norms[s], 1), :].astype(jnp.bfloat16)
            left.append(tile[tiles[s]] * scale)
            row = pl.multiple_of((index & 15) * BLOCK, BLOCK)
            right.append(feat[index >> 4, pl.ds(row, BLOCK), :])
        return total + jnp.dot(
            jnp.concatenate(left, axis=1), jnp.concatenate(right, axis=0),
            preferred_element_type=jnp.float32,
        )

    def make(out, base):
        def rows(d, carry):
            total = lax.fori_loop(
                start[base + d], start[base + d + 1], add_group, jnp.zeros((BLOCK, WIDTH), jnp.float32)
            )
            out[pl.ds(pl.multiple_of(d * BLOCK, BLOCK), BLOCK), :] = total.astype(out.dtype)
            return carry

        lax.fori_loop(0, DST_BLK // 2, rows, 0)

    make(sent, 0)
    make(kept, DST_BLK // 2)


def sum_tiles(lists, pieces, own_tiles, other_tiles):
    smem = pl.BlockSpec(memory_space=pltpu.SMEM)
    anywhere = pl.BlockSpec(memory_space=pl.ANY)
    vmem = pl.BlockSpec(memory_space=pltpu.VMEM)
    half = DST_BLK // 2 * BLOCK
    return pl.pallas_call(
        sum_kernel,
        out_shape=(
            jax.ShapeDtypeStruct((half, WIDTH), jnp.float32),
            jax.ShapeDtypeStruct((half, WIDTH), jnp.float32),
        ),
        in_specs=[smem] * 4 + [anywhere] * 10,
        out_specs=(vmem, vmem),
        scratch_shapes=[
            pltpu.VMEM((8, HALF_ROWS, WIDTH), jnp.bfloat16),
            pltpu.VMEM((256, BLOCK, BLOCK), jnp.bfloat16),
            pltpu.VMEM((136, BLOCK), jnp.float32),
            pltpu.SemaphoreType.DMA((10,)),
        ],
        compiler_params=pltpu.CompilerParams(vmem_limit_bytes=32 * MIB),
        cost_estimate=pl.CostEstimate(flops=2 * 10**9, bytes_accessed=20 * 10**6, transcendentals=0),
    )(*lists, *pieces, own_tiles, other_tiles)


def gather_features(features, src_norm, rep):
    mine = lax.dynamic_slice_in_dim(features, rep * BLOCK, BLOCK, 0)
    my_norm = lax.dynamic_slice_in_dim(src_norm, rep * BLOCK, BLOCK, 0)
    norm_rows = jnp.zeros((16, WIDTH), jnp.bfloat16).at[0, :BLOCK].set(my_norm)
    shard = jnp.concatenate([mine, norm_rows], axis=0)
    at = {0: shard}
    for step in (1, -1, 2, -2):
        at[step] = move(shard, from_z(step))
    far = move(jnp.concatenate([at[1], at[2]], axis=0), from_z(2))
    at[3], at[4] = far[:144], far[144:]
    at[-3] = move(at[-1], from_z(-2))
    line = [at[k] for k in (0, 1, 2, 3, 4, -3, -2, -1)]
    line = jnp.concatenate(
        [s[:BLOCK] for s in line] + [s[BLOCK : BLOCK + 1] for s in line]
        + [jnp.zeros((8, WIDTH), jnp.bfloat16)], axis=0
    )
    around = [line] + [move(line, from_second(step)) for step in (1, 2, 3)]
    cut = NZ * BLOCK
    halves = [
        jnp.concatenate([a[:cut], b[:cut], a[cut : cut + 8], b[cut : cut + 8]], axis=0)
        for a, b in (around[:2], around[2:])
    ]
    up_0 = move(halves[0], from_third(1))
    down_1 = move(halves[1], from_third(-1))
    up_1 = move(halves[1], from_third(1))
    down_0 = move(halves[0], from_third(-1))
    across_0 = move(up_0, from_third(1))
    across_1 = move(down_1, from_third(-1))
    return [halves[0], halves[1], up_0, up_1, across_0, across_1, down_0, down_1]


def body(features, src_norm, dst_norm, src_block, dst_block, counts, weight, out_bias):
    rep = lax.axis_index("rep")
    col = lax.axis_index("col")
    x, y, z = col // (NY * NZ), (col // NZ) % NY, col % NZ
    swap = [(0, 1), (1, 0)]
    ids = jnp.concatenate([src_block.reshape(1, -1), dst_block.reshape(1, -1)], axis=0)
    other_ids = lax.ppermute(ids, "rep", swap)
    place = jnp.stack([z, jnp.where(rep == 0, y, x), jnp.where(rep == 0, x, y), rep]).astype(jnp.int32)
    lists = sort_blocks(
        place, jnp.concatenate([ids[0], other_ids[0]]), jnp.concatenate([ids[1], other_ids[1]])
    )
    own_tiles = counts.reshape(-1, BLOCK, BLOCK).astype(jnp.bfloat16)
    other_tiles = lax.ppermute(own_tiles, "rep", swap)
    pieces = gather_features(features, src_norm, rep)
    sent, kept = sum_tiles(lists, pieces, own_tiles, other_tiles)
    half_rows = kept.shape[0]
    own_norm = lax.dynamic_slice_in_dim(dst_norm, rep * half_rows, half_rows, 0)
    aggregate = (kept + lax.ppermute(sent, "rep", swap)) * own_norm[:, None]
    hidden = aggregate.astype(jnp.bfloat16)
    result = jnp.dot(hidden, weight, preferred_element_type=jnp.float32) + out_bias.astype(jnp.float32)
    return jax.nn.relu(result).astype(jnp.bfloat16)


def solution(mesh):
    placed = (
        P("col", None),
        P("col"),
        P("col"),
        P("col", "rep", None),
        P("col", "rep", None),
        P("col", "rep", None, None, None),
        P(),
        P(),
    )
    return jax.shard_map(
        body, mesh=mesh, in_specs=placed, out_specs=P(("col", "rep"), None), check_vma=False
    )
```

```python
import functools

import jax
import jax.numpy as jnp
from jax import lax
from jax.experimental import pallas as pl
from jax.experimental.pallas import tpu as pltpu
from jax.sharding import PartitionSpec as P

BLOCK = 128
DST_BLK = 32
WIDTH = 256
NX, NY, NZ = 4, 4, 8
SHARD = 2 * BLOCK + 16
LINE = 8 * BLOCK + 16
DEPTH = 64
UNROLL = 4
SEGMENTS = 8
SEG_SLOTS = 2 * BLOCK + UNROLL
PACKED = 2 * BLOCK + SEGMENTS * (UNROLL - 1)
DST_ROWS = DST_BLK * BLOCK
HALF = DST_ROWS // 2
MIB = 1024 * 1024


def device(x, y, z, r):
    return (((x % NX) * NY + (y % NY)) * NZ + (z % NZ)) * 2 + r


def from_z(step):
    return [
        (device(x, y, z - step if r else z + step % 4, r), device(x, y, z, r))
        for x in range(NX) for y in range(NY) for z in range(NZ) for r in range(2)
    ]


def from_second(step):
    return [
        (device(x, y + step, z, 0) if r == 0 else device(x + step, y, z, 1), device(x, y, z, r))
        for x in range(NX) for y in range(NY) for z in range(NZ) for r in range(2)
    ]


def from_third(step):
    return [
        (device(x + step, y, z, 0) if r == 0 else device(x, y + step, z, 1), device(x, y, z, r))
        for x in range(NX) for y in range(NY) for z in range(NZ) for r in range(2)
    ]


def move(value, pairs):
    return lax.ppermute(value, ("col", "rep"), pairs)


def line_kernel(a, b, c, d, own, slots, line):
    cut = 2 * BLOCK
    norms = []
    for k, shard in enumerate((a, b, c, d)):
        line[pl.ds(k * cut, cut), :] = shard[pl.ds(0, cut), :]
        norms.append(shard[pl.ds(cut, 16), :][:1].astype(jnp.float32))
    rows = jnp.concatenate(norms + [jnp.zeros((12, WIDTH), jnp.float32)], axis=0)
    line[pl.ds(8 * BLOCK, 16), :] = rows.astype(jnp.bfloat16)


def make_line(shards, own, slots):
    vmem = pl.BlockSpec(memory_space=pltpu.VMEM)
    return pl.pallas_call(
        line_kernel,
        out_shape=jax.ShapeDtypeStruct((LINE, WIDTH), jnp.bfloat16),
        in_specs=[vmem] * 4 + [pl.BlockSpec(memory_space=pltpu.HBM), pl.BlockSpec(memory_space=pl.ANY)],
        out_specs=vmem,
        compiler_params=pltpu.CompilerParams(vmem_limit_bytes=4 * MIB),
    )(*shards, own, slots)


def sort_kernel(codes, base, slots, count, listed):
    def clear(k, carry):
        count[k] = 0
        return carry

    lax.fori_loop(0, SEGMENTS, clear, 0)

    def put(i, carry):
        for u in range(4):
            code = codes[4 * i + u]
            segment = (code >> 26) & 15
            at = count[segment]
            listed[segment * SEG_SLOTS + at] = code
            count[segment] = at + (code >> 30)
        return carry

    lax.fori_loop(0, 64, put, 0)

    def squeeze(k, at):
        base[k] = at
        size = count[k]
        for u in range(UNROLL - 1):
            listed[k * SEG_SLOTS + size + u] = 4 << 21
        groups = (size + (UNROLL - 1)) >> 2

        def copy(g, carry):
            for u in range(UNROLL):
                slots[(at + g) * UNROLL + u] = listed[k * SEG_SLOTS + g * UNROLL + u]
            return carry

        lax.fori_loop(0, groups, copy, 0)
        return at + groups

    base[SEGMENTS] = lax.fori_loop(0, SEGMENTS, squeeze, 0)


def sort_codes(codes):
    smem = pl.BlockSpec(memory_space=pltpu.SMEM)
    return pl.pallas_call(
        sort_kernel,
        out_shape=(
            jax.ShapeDtypeStruct((SEGMENTS + 1,), jnp.int32),
            jax.ShapeDtypeStruct((PACKED,), jnp.int32),
        ),
        in_specs=[smem],
        out_specs=(smem, smem),
        scratch_shapes=[
            pltpu.SMEM((SEGMENTS,), jnp.int32),
            pltpu.SMEM((SEGMENTS * SEG_SLOTS,), jnp.int32),
        ],
        compiler_params=pltpu.CompilerParams(vmem_limit_bytes=2 * MIB),
    )(codes)


def pack_kernel(base, slots, own, other, packed, tile, in_sem):
    total = base[SEGMENTS]

    def fetch(g):
        slot = lax.rem(g, DEPTH // UNROLL)
        for u in range(UNROLL):
            e = slots[g * UNROLL + u] & 255

            @pl.when(e < BLOCK)
            def _():
                pltpu.make_async_copy(own.at[e], tile.at[slot, u], in_sem.at[slot, u]).start()

            @pl.when(e >= BLOCK)
            def _():
                pltpu.make_async_copy(other.at[e - BLOCK], tile.at[slot, u], in_sem.at[slot, u]).start()

    def begin(g, carry):
        fetch(g)
        return carry

    ahead = DEPTH // UNROLL - 1
    lax.fori_loop(0, jnp.minimum(total, ahead), begin, 0)

    def step(g, carry):
        slot = lax.rem(g, DEPTH // UNROLL)

        @pl.when(g + ahead < total)
        def _():
            fetch(g + ahead)

        for u in range(UNROLL):
            pltpu.make_async_copy(own.at[0], tile.at[slot, u], in_sem.at[slot, u]).wait()

        packed[g] = tile[slot].astype(jnp.float32).astype(jnp.bfloat16)
        return carry

    lax.fori_loop(0, total, step, 0)


def pack_tiles(lists, own, other):
    smem = pl.BlockSpec(memory_space=pltpu.SMEM)
    hbm = pl.BlockSpec(memory_space=pltpu.HBM)
    ring = (DEPTH // UNROLL, UNROLL, BLOCK, BLOCK)
    return pl.pallas_call(
        pack_kernel,
        out_shape=jax.ShapeDtypeStruct((PACKED // UNROLL, UNROLL, BLOCK, BLOCK), jnp.bfloat16),
        in_specs=[smem, smem, hbm, hbm],
        out_specs=pl.BlockSpec(memory_space=pltpu.VMEM),
        scratch_shapes=[pltpu.VMEM(ring, jnp.int32), pltpu.SemaphoreType.DMA(ring[:2])],
        compiler_params=pltpu.CompilerParams(vmem_limit_bytes=16 * MIB),
        cost_estimate=pl.CostEstimate(flops=10**6, bytes_accessed=20 * 10**6, transcendentals=0),
    )(*lists, own, other)


def halves_kernel(a, b, c, d, packed, low, high):
    for out, lines in ((low, (a, b)), (high, (c, d))):
        for k, line in enumerate(lines):
            out[pl.ds(k * LINE, LINE), :] = line[...]


def make_halves(lines, packed):
    vmem = pl.BlockSpec(memory_space=pltpu.VMEM)
    half = jax.ShapeDtypeStruct((2 * LINE, WIDTH), jnp.bfloat16)
    return pl.pallas_call(
        halves_kernel,
        out_shape=(half, half),
        in_specs=[vmem] * 4 + [pl.BlockSpec(memory_space=pl.ANY)],
        out_specs=(vmem, vmem),
        compiler_params=pltpu.CompilerParams(vmem_limit_bytes=8 * MIB),
    )(*lines, packed)


def sum_kernel(ids, before, *refs):
    base, slots, packed = refs[:3]
    pieces = refs[3 : 3 + len(ids)]
    refs = refs[3 + len(ids) :]
    if before:
        earlier, refs = refs[0], refs[1:]
    if len(refs) > 2:
        sent, kept, norm, total = refs
    else:
        total, norm = refs
    if before:
        total[...] = earlier[...]
    else:
        total[...] = jnp.zeros_like(total)
    for i, piece in enumerate(pieces):
        for line in range(2):
            for half in range(2):
                rows = piece[pl.ds(line * LINE + 8 * BLOCK, 16), pl.ds(half * BLOCK, BLOCK)]
                norm[pl.ds(32 * i + 16 * half + 8 * line, 8), :] = rows.astype(jnp.float32)[:8]
    for i, (k, piece) in enumerate(zip(ids, pieces)):
        first, last = base[k], base[k + 1]

        def add(g, groups, i=i, piece=piece):
            found = []
            for u in range(UNROLL * groups):
                code = slots[UNROLL * g + u]
                scale = norm[pl.ds(32 * i + ((code >> 21) & 31), 1), :]
                row = pl.multiple_of(((code >> 13) & 255) * 16, 16)
                found.append((
                    pl.multiple_of(((code >> 8) & 31) * BLOCK, BLOCK),
                    jnp.dot(
                        packed[g + u // UNROLL, u % UNROLL] * scale.astype(jnp.bfloat16),
                        piece[pl.ds(row, BLOCK), :], preferred_element_type=jnp.float32,
                    ),
                ))
            for at, product in found:
                total[pl.ds(at, BLOCK), :] += product

        def pair(j, carry, first=first, add=add):
            add(first + 2 * j, 2)
            return carry

        lax.fori_loop(0, (last - first) >> 1, pair, 0)

        @pl.when(((last - first) & 1) == 1)
        def _(last=last, add=add):
            add(last - 1, 1)

    if len(refs) > 2:
        sent[...] = total[pl.ds(0, HALF), :].astype(sent.dtype)
        kept[...] = total[pl.ds(HALF, HALF), :]


def sum_tiles(lists, pieces, earlier=None, last=False):
    smem = pl.BlockSpec(memory_space=pltpu.SMEM)
    vmem = pl.BlockSpec(memory_space=pltpu.VMEM)
    ids = tuple(pieces)
    before = [] if earlier is None else [earlier]
    whole = jax.ShapeDtypeStruct((DST_ROWS, WIDTH), jnp.float32)
    ends = tuple(jax.ShapeDtypeStruct((HALF, WIDTH), t) for t in (jnp.bfloat16, jnp.float32))
    norm = pltpu.VMEM((32 * len(ids), BLOCK), jnp.float32)
    return pl.pallas_call(
        functools.partial(sum_kernel, ids, bool(before)),
        out_shape=ends if last else whole,
        in_specs=[smem] * 2 + [vmem] * (1 + len(ids) + len(before)),
        out_specs=(vmem, vmem) if last else vmem,
        scratch_shapes=[norm] + ([pltpu.VMEM(whole.shape, whole.dtype)] if last else []),
        compiler_params=pltpu.CompilerParams(vmem_limit_bytes=8 * MIB),
        cost_estimate=pl.CostEstimate(flops=4 * 10**8, bytes_accessed=8 * 10**6, transcendentals=0),
    )(*lists, *pieces.values(), *before)


def finish_kernel(kept, received, scale, weight, bias, out, buffer, sems):
    step = HALF // 8
    copies = []
    for i in range(8):
        rows = pl.ds(i * step, step)
        factor = jnp.concatenate([scale[rows, :]] * 2, axis=1)
        aggregate = (kept[rows, :] + received[rows, :].astype(jnp.float32)) * factor
        result = jnp.dot(
            aggregate.astype(jnp.bfloat16), weight[...], preferred_element_type=jnp.float32
        ) + bias[...]
        buffer[rows, :] = jnp.maximum(result, 0.0).astype(jnp.bfloat16)
        copies.append(pltpu.make_async_copy(buffer.at[rows], out.at[rows], sems.at[i]))
        copies[-1].start()
    for copy in copies:
        copy.wait()


def finish(kept, received, scale, weight, bias):
    vmem = pl.BlockSpec(memory_space=pltpu.VMEM)
    return pl.pallas_call(
        finish_kernel,
        out_shape=jax.ShapeDtypeStruct((HALF, WIDTH), jnp.bfloat16),
        in_specs=[vmem] * 5,
        out_specs=pl.BlockSpec(memory_space=pl.ANY),
        scratch_shapes=[pltpu.VMEM((HALF, WIDTH), jnp.bfloat16), pltpu.SemaphoreType.DMA((8,))],
        compiler_params=pltpu.CompilerParams(vmem_limit_bytes=12 * MIB),
        cost_estimate=pl.CostEstimate(flops=3 * 10**8, bytes_accessed=6 * 10**6, transcendentals=0),
    )(kept, received, scale, weight, bias)


def encode(src, dst, place):
    z, second, third, rep = place
    entry = jnp.arange(2 * BLOCK, dtype=jnp.int32)
    p = src >> 1
    dz = ((p & 7) - z) & 7
    px, py = p >> 5, (p >> 3) & 3
    pa = jnp.where(rep == 0, py, px)
    pb = jnp.where(rep == 0, px, py)
    shard = jnp.where(rep == 0, dz, 8 - dz) & 3
    da, db = (pa - second) & 3, (pb - third) & 3
    line = da & 1
    d = (dst + 16 * (1 - rep)) & 31
    segment = db * 2 + (da >> 1)
    row16 = line * (LINE // 16) + shard * 16 + (src & 1) * 8
    scale = (src & 1) * 16 + line * 8 + shard
    valid = jnp.where((dz >> 2) == rep, 1, 0)
    return entry | (d << 8) | (row16 << 13) | (scale << 21) | (segment << 26) | (valid << 30)


def gather_shards(features, src_norm):
    norm_rows = jnp.zeros((16, WIDTH), jnp.bfloat16).at[0].set(src_norm)
    shard = jnp.concatenate([features, norm_rows], axis=0)
    return [move(shard, from_z(step)) for step in (4, 1, 2, 3)]


def body(features, src_norm, dst_norm, src_block, dst_block, counts, weight, out_bias):
    rep = lax.axis_index("rep")
    col = lax.axis_index("col")
    x, y, z = col // (NY * NZ), (col // NZ) % NY, col % NZ
    swap = [(0, 1), (1, 0)]
    own = counts.reshape(-1, BLOCK, BLOCK)
    other = lax.ppermute(own, "rep", swap)
    ids = jnp.concatenate([src_block.reshape(1, -1), dst_block.reshape(1, -1)], axis=0)
    all_ids = lax.all_gather(ids, "rep")
    both = jnp.concatenate([ids, jnp.where(rep == 0, all_ids[1], all_ids[0])], axis=1)
    place = (z, jnp.where(rep == 0, y, x), jnp.where(rep == 0, x, y), rep)
    base, slots = sort_codes(encode(both[0], both[1], place))
    line_0 = make_line(gather_shards(features, src_norm), other, slots)
    lines = [line_0] + [move(line_0, from_second(step)) for step in (1, 2, 3)]
    packed = pack_tiles((base, slots), own, other)
    lists = (base, slots, packed)
    half_0, half_1 = make_halves(lines, packed)
    up_0 = move(half_0, from_third(1))
    down_1 = move(half_1, from_third(-1))
    up_1 = move(half_1, from_third(1))
    down_0 = move(half_0, from_third(-1))
    across_0 = move(up_0, from_third(1))
    across_1 = move(down_1, from_third(-1))
    total = sum_tiles(lists, {0: half_0, 1: half_1})
    total = sum_tiles(lists, {2: up_0, 7: down_1, 3: up_1, 6: down_0}, total)
    sent, kept = sum_tiles(lists, {4: across_0, 5: across_1}, total, True)
    received = lax.ppermute(sent, "rep", swap)
    own_norm = lax.dynamic_slice_in_dim(dst_norm, rep * HALF, HALF, 0)
    scale = jnp.broadcast_to(own_norm[:, None], (HALF, BLOCK))
    return finish(kept, received, scale, weight, out_bias.astype(jnp.float32).reshape(1, -1))


def solution(mesh):
    placed = (
        P("col", None),
        P("col"),
        P("col"),
        P("col", "rep", None),
        P("col", "rep", None),
        P("col", "rep", None, None, None),
        P(),
        P(),
    )
    return jax.shard_map(
        body, mesh=mesh, in_specs=placed, out_specs=P(("col", "rep"), None), check_vma=False
    )
```

```python
import functools

import jax
import jax.numpy as jnp
from jax import lax
from jax.experimental import pallas as pl
from jax.experimental.pallas import tpu as pltpu
from jax.sharding import PartitionSpec as P

BLOCK = 128
DST_BLK = 32
WIDTH = 256
NX, NY, NZ = 4, 4, 8
SHARD = 2 * BLOCK + 16
LINE = 8 * BLOCK + 16
DEPTH = 64
UNROLL = 4
SEGMENTS = 16
SEG_SLOTS = 2 * BLOCK + UNROLL
PACKED = 2 * BLOCK + SEGMENTS * (UNROLL - 1)
DST_ROWS = DST_BLK * BLOCK
HALF = DST_ROWS // 2
MIB = 1024 * 1024


def device(x, y, z, r):
    return (((x % NX) * NY + (y % NY)) * NZ + (z % NZ)) * 2 + r


def from_z(step):
    return [
        (device(x, y, 4 * r + (z + step) % 4, z // 4), device(x, y, z, r))
        for x in range(NX) for y in range(NY) for z in range(NZ) for r in range(2)
        if step or r != z // 4
    ]


def from_beside(step):
    return [
        (device(x, y, z - step if r else z + step, r), device(x, y, z, r))
        for x in range(NX) for y in range(NY) for z in range(NZ) for r in range(2)
    ]


def from_second(step):
    return [
        (device(x, y + step, z, 0) if r == 0 else device(x + step, y, z, 1), device(x, y, z, r))
        for x in range(NX) for y in range(NY) for z in range(NZ) for r in range(2)
    ]


def from_third(step):
    return [
        (device(x + step, y, z, 0) if r == 0 else device(x, y + step, z, 1), device(x, y, z, r))
        for x in range(NX) for y in range(NY) for z in range(NZ) for r in range(2)
    ]


def move(value, pairs):
    return lax.ppermute(value, ("col", "rep"), pairs)


def line_kernel(keep, own, b, c, d, a, swapped, codes, line):
    cut = 2 * BLOCK
    norms = []
    for k, shard in enumerate((a, b, c, d)):
        rows, norm = shard[pl.ds(0, cut), :], shard[pl.ds(cut, 16), :]
        if k == 0:
            rows = jnp.where(keep[0] != 0, own[pl.ds(0, cut), :], rows)
            norm = jnp.where(keep[0] != 0, own[pl.ds(cut, 16), :], norm)
        line[pl.ds(k * cut, cut), :] = rows
        norms.append(norm[:1].astype(jnp.float32))
    rows = jnp.concatenate(norms + [jnp.zeros((12, WIDTH), jnp.float32)], axis=0)
    line[pl.ds(8 * BLOCK, 16), :] = rows.astype(jnp.bfloat16)


def make_line(keep, shards, own, slots):
    vmem = pl.BlockSpec(memory_space=pltpu.VMEM)
    return pl.pallas_call(
        line_kernel,
        out_shape=jax.ShapeDtypeStruct((LINE, WIDTH), jnp.bfloat16),
        in_specs=[pl.BlockSpec(memory_space=pltpu.SMEM)] + [vmem] * 5
        + [pl.BlockSpec(memory_space=pltpu.HBM), pl.BlockSpec(memory_space=pl.ANY)],
        out_specs=vmem,
        compiler_params=pltpu.CompilerParams(vmem_limit_bytes=4 * MIB),
    )(keep, *shards, own, slots)


def sort_codes(codes, base, slots, count, listed):
    def clear(k, carry):
        count[k] = 0
        return carry

    lax.fori_loop(0, SEGMENTS, clear, 0)

    def put(i, carry):
        for u in range(4):
            code = codes[4 * i + u]
            segment = (code >> 26) & 15
            at = count[segment]
            listed[segment * SEG_SLOTS + at] = code
            count[segment] = at + (code >> 30)
        return carry

    lax.fori_loop(0, 64, put, 0)

    def squeeze(k, at):
        base[k] = at
        size = count[k]
        for u in range(UNROLL - 1):
            listed[k * SEG_SLOTS + size + u] = 4 << 21
        groups = (size + (UNROLL - 1)) >> 2

        def copy(g, carry):
            for u in range(UNROLL):
                slots[(at + g) * UNROLL + u] = listed[k * SEG_SLOTS + g * UNROLL + u]
            return carry

        lax.fori_loop(0, groups, copy, 0)
        return at + groups

    base[SEGMENTS] = lax.fori_loop(0, SEGMENTS, squeeze, 0)


def pack_kernel(codes, own, other, base, slots, packed, count, listed, tile, in_sem):
    sort_codes(codes, base, slots, count, listed)
    total = base[SEGMENTS]

    def fetch(g):
        slot = lax.rem(g, DEPTH // UNROLL)
        for u in range(UNROLL):
            e = slots[g * UNROLL + u] & 255

            @pl.when(e < BLOCK)
            def _():
                pltpu.make_async_copy(own.at[e], tile.at[slot, u], in_sem.at[slot, u]).start()

            @pl.when(e >= BLOCK)
            def _():
                pltpu.make_async_copy(other.at[e - BLOCK], tile.at[slot, u], in_sem.at[slot, u]).start()

    def begin(g, carry):
        fetch(g)
        return carry

    ahead = DEPTH // UNROLL - 1
    lax.fori_loop(0, jnp.minimum(total, ahead), begin, 0)

    def step(g, carry):
        slot = lax.rem(g, DEPTH // UNROLL)

        @pl.when(g + ahead < total)
        def _():
            fetch(g + ahead)

        for u in range(UNROLL):
            pltpu.make_async_copy(own.at[0], tile.at[slot, u], in_sem.at[slot, u]).wait()

        packed[g] = tile[slot].astype(jnp.float32).astype(jnp.bfloat16)
        return carry

    lax.fori_loop(0, total, step, 0)


def pack_tiles(codes, own, other):
    smem = pl.BlockSpec(memory_space=pltpu.SMEM)
    hbm = pl.BlockSpec(memory_space=pltpu.HBM)
    ring = (DEPTH // UNROLL, UNROLL, BLOCK, BLOCK)
    return pl.pallas_call(
        pack_kernel,
        out_shape=(
            jax.ShapeDtypeStruct((SEGMENTS + 1,), jnp.int32),
            jax.ShapeDtypeStruct((PACKED,), jnp.int32),
            jax.ShapeDtypeStruct((PACKED // UNROLL, UNROLL, BLOCK, BLOCK), jnp.bfloat16),
        ),
        in_specs=[smem, hbm, hbm],
        out_specs=(smem, smem, pl.BlockSpec(memory_space=pltpu.VMEM)),
        scratch_shapes=[
            pltpu.SMEM((SEGMENTS,), jnp.int32),
            pltpu.SMEM((SEGMENTS * SEG_SLOTS,), jnp.int32),
            pltpu.VMEM(ring, jnp.int32),
            pltpu.SemaphoreType.DMA(ring[:2]),
        ],
        compiler_params=pltpu.CompilerParams(vmem_limit_bytes=20 * MIB),
        cost_estimate=pl.CostEstimate(flops=10**6, bytes_accessed=20 * 10**6, transcendentals=0),
    )(codes, own, other)


def join_kernel(odd, a, b, c, d, packed, single, double):
    double[pl.ds(0, LINE), :] = b[...]
    double[pl.ds(LINE, LINE), :] = c[...]

    @pl.when(odd[0] == 0)
    def _():
        single[...] = a[...]

    @pl.when(odd[0] != 0)
    def _():
        single[...] = d[...]


def join_lines(odd, lines, packed):
    vmem = pl.BlockSpec(memory_space=pltpu.VMEM)
    return pl.pallas_call(
        join_kernel,
        out_shape=tuple(jax.ShapeDtypeStruct((n * LINE, WIDTH), jnp.bfloat16) for n in (1, 2)),
        in_specs=[pl.BlockSpec(memory_space=pltpu.SMEM)] + [vmem] * 4 + [pl.BlockSpec(memory_space=pl.ANY)],
        out_specs=(vmem, vmem),
        compiler_params=pltpu.CompilerParams(vmem_limit_bytes=8 * MIB),
    )(odd, *lines, packed)


def sum_kernel(ids, before, *refs):
    base, slots, packed = refs[:3]
    pieces = refs[3 : 3 + len(ids)]
    refs = refs[3 + len(ids) :]
    if before:
        earlier, refs = refs[0], refs[1:]
    if len(refs) > 2:
        sent, kept, norm, total = refs
    else:
        total, norm = refs
    if before:
        total[...] = earlier[...]
    else:
        total[...] = jnp.zeros_like(total)
    for i, piece in enumerate(pieces):
        for line in range(piece.shape[0] // LINE):
            for half in range(2):
                rows = piece[pl.ds(line * LINE + 8 * BLOCK, 16), pl.ds(half * BLOCK, BLOCK)]
                norm[pl.ds(32 * i + 16 * half + 8 * line, 8), :] = rows.astype(jnp.float32)[:8]
    for i, (k, piece) in enumerate(zip(ids, pieces)):
        first, last = base[k], base[k + 1]

        def add(g, groups, i=i, piece=piece):
            found = []
            for u in range(UNROLL * groups):
                code = slots[UNROLL * g + u]
                scale = norm[pl.ds(32 * i + ((code >> 21) & 31), 1), :]
                row = pl.multiple_of(((code >> 13) & 255) * 16, 16)
                found.append((
                    pl.multiple_of(((code >> 8) & 31) * BLOCK, BLOCK),
                    jnp.dot(
                        packed[g + u // UNROLL, u % UNROLL] * scale.astype(jnp.bfloat16),
                        piece[pl.ds(row, BLOCK), :], preferred_element_type=jnp.float32,
                    ),
                ))
            for at, product in found:
                total[pl.ds(at, BLOCK), :] += product

        def pair(j, carry, first=first, add=add):
            add(first + 2 * j, 2)
            return carry

        lax.fori_loop(0, (last - first) >> 1, pair, 0)

        @pl.when(((last - first) & 1) == 1)
        def _(last=last, add=add):
            add(last - 1, 1)

    if len(refs) > 2:
        sent[...] = total[pl.ds(0, HALF), :].astype(sent.dtype)
        kept[...] = total[pl.ds(HALF, HALF), :]


def sum_tiles(lists, pieces, earlier=None, last=False):
    smem = pl.BlockSpec(memory_space=pltpu.SMEM)
    vmem = pl.BlockSpec(memory_space=pltpu.VMEM)
    ids = tuple(pieces)
    before = [] if earlier is None else [earlier]
    whole = jax.ShapeDtypeStruct((DST_ROWS, WIDTH), jnp.float32)
    ends = tuple(jax.ShapeDtypeStruct((HALF, WIDTH), t) for t in (jnp.bfloat16, jnp.float32))
    norm = pltpu.VMEM((32 * len(ids), BLOCK), jnp.float32)
    return pl.pallas_call(
        functools.partial(sum_kernel, ids, bool(before)),
        out_shape=ends if last else whole,
        in_specs=[smem] * 2 + [vmem] * (1 + len(ids) + len(before)),
        out_specs=(vmem, vmem) if last else vmem,
        scratch_shapes=[norm] + ([pltpu.VMEM(whole.shape, whole.dtype)] if last else []),
        compiler_params=pltpu.CompilerParams(vmem_limit_bytes=8 * MIB),
        cost_estimate=pl.CostEstimate(flops=4 * 10**8, bytes_accessed=8 * 10**6, transcendentals=0),
    )(*lists, *pieces.values(), *before)


def finish_kernel(kept, received, scale, weight, bias, out, buffer, sems):
    step = HALF // 8
    copies = []
    for i in range(8):
        rows = pl.ds(i * step, step)
        factor = jnp.concatenate([scale[rows, :]] * 2, axis=1)
        aggregate = (kept[rows, :] + received[rows, :].astype(jnp.float32)) * factor
        result = jnp.dot(
            aggregate.astype(jnp.bfloat16), weight[...], preferred_element_type=jnp.float32
        ) + bias[...]
        buffer[rows, :] = jnp.maximum(result, 0.0).astype(jnp.bfloat16)
        copies.append(pltpu.make_async_copy(buffer.at[rows], out.at[rows], sems.at[i]))
        copies[-1].start()
    for copy in copies:
        copy.wait()


def finish(kept, received, scale, weight, bias):
    vmem = pl.BlockSpec(memory_space=pltpu.VMEM)
    return pl.pallas_call(
        finish_kernel,
        out_shape=jax.ShapeDtypeStruct((HALF, WIDTH), jnp.bfloat16),
        in_specs=[vmem] * 5,
        out_specs=pl.BlockSpec(memory_space=pl.ANY),
        scratch_shapes=[pltpu.VMEM((HALF, WIDTH), jnp.bfloat16), pltpu.SemaphoreType.DMA((8,))],
        compiler_params=pltpu.CompilerParams(vmem_limit_bytes=12 * MIB),
        cost_estimate=pl.CostEstimate(flops=3 * 10**8, bytes_accessed=6 * 10**6, transcendentals=0),
    )(kept, received, scale, weight, bias)


OWN_0, OWN_12, OWN_3 = 0, 1, 2
UP, UP_12, UP_Z = 4, 5, 6
FAR, FAR_12, FAR_Z = 8, 9, 10
DOWN, DOWN_12, DOWN_Z = 12, 13, 14


def encode(src, dst, place):
    z, second, third, rep = place
    entry = jnp.arange(2 * BLOCK, dtype=jnp.int32)
    p = src >> 1
    px, py, pz = p >> 5, (p >> 3) & 3, p & 7
    pa = jnp.where(rep == 0, py, px)
    pb = jnp.where(rep == 0, px, py)
    da, db = (pa - second) & 3, (pb - third) & 3
    double = (da == 1) | (da == 2)
    beside = (db != 0) & (da == jnp.where((z & 1) == 0, 3, 0))
    own_kind = jnp.where(double, 1, jnp.where(da == 0, 0, 2))
    far_kind = jnp.where(double, 1, jnp.where(beside, 2, 0))
    segment = db * 4 + jnp.where(db == 0, own_kind, far_kind)
    line = jnp.where(da == 2, 1, 0)
    z_of = jnp.where(beside, jnp.where((rep == 0) == (db != 3), z + 1, z - 1), z)
    shard = (pz - z_of) & 3
    d = (dst + 16 * (1 - rep)) & 31
    row16 = line * (LINE // 16) + shard * 16 + (src & 1) * 8
    scale = (src & 1) * 16 + line * 8 + shard
    valid = jnp.where((pz >> 2) == rep, 1, 0)
    return entry | (d << 8) | (row16 << 13) | (scale << 21) | (segment << 26) | (valid << 30)


def gather_shards(features, src_norm):
    norm_rows = jnp.broadcast_to(src_norm, (16, WIDTH))
    shard = jnp.concatenate([features, norm_rows], axis=0)
    near = [move(shard, from_z(step)) for step in (1, 2, 3)]
    return [shard, *near, move(shard, from_z(0))]


def body(features, src_norm, dst_norm, src_block, dst_block, counts, weight, out_bias):
    rep = lax.axis_index("rep")
    col = lax.axis_index("col")
    x, y, z = col // (NY * NZ), (col // NZ) % NY, col % NZ
    swap = [(0, 1), (1, 0)]
    own = counts.reshape(-1, BLOCK, BLOCK)
    other = lax.ppermute(own, "rep", swap)
    ids = jnp.concatenate([src_block.reshape(1, -1), dst_block.reshape(1, -1)], axis=0)
    all_ids = lax.all_gather(ids, "rep")
    both = jnp.concatenate([ids, jnp.where(rep == 0, all_ids[1], all_ids[0])], axis=1)
    place = (z, jnp.where(rep == 0, y, x), jnp.where(rep == 0, x, y), rep)
    codes = encode(both[0], both[1], place)
    line_0 = make_line(
        jnp.where(z // 4 == rep, 1, 0).astype(jnp.int32).reshape(1), gather_shards(features, src_norm), other, codes)
    lines = [line_0] + [move(line_0, from_second(step)) for step in (1, 2, 3)]
    lists = pack_tiles(codes, own, other)
    single, double = join_lines((z & 1).astype(jnp.int32).reshape(1), lines, lists[2])
    up = move(single, from_third(1))
    down_12 = move(double, from_third(-1))
    up_12 = move(double, from_third(1))
    down = move(single, from_third(-1))
    up_z = move(up, from_beside(1))
    down_z = move(down, from_beside(-1))
    far = move(up, from_third(1))
    far_12 = move(down_12, from_third(-1))
    far_z = move(up_z, from_third(1))
    total = sum_tiles(lists, {OWN_0: lines[0], OWN_12: double, OWN_3: lines[3]})
    near = {UP: up, UP_Z: up_z, DOWN_12: down_12, DOWN: down, UP_12: up_12, FAR: far}
    total = sum_tiles(lists, near, total)
    sent, kept = sum_tiles(lists, {FAR_12: far_12, FAR_Z: far_z, DOWN_Z: down_z}, total, True)
    received = lax.ppermute(sent, "rep", swap)
    own_norm = lax.dynamic_slice_in_dim(dst_norm, rep * HALF, HALF, 0)
    scale = jnp.broadcast_to(own_norm[:, None], (HALF, BLOCK))
    return finish(kept, received, scale, weight, out_bias.astype(jnp.float32).reshape(1, -1))


def solution(mesh):
    placed = (
        P("col", None),
        P("col"),
        P("col"),
        P("col", "rep", None),
        P("col", "rep", None),
        P("col", "rep", None, None, None),
        P(),
        P(),
    )
    return jax.shard_map(
        body, mesh=mesh, in_specs=placed, out_specs=P(("col", "rep"), None), check_vma=False
    )
```

```python
import functools

import jax
import jax.numpy as jnp
from jax import lax
from jax.experimental import pallas as pl
from jax.experimental.pallas import tpu as pltpu
from jax.sharding import PartitionSpec as P

BLOCK = 128
DST_BLK = 32
WIDTH = 256
NX, NY, NZ = 4, 4, 8
SHARD = 2 * BLOCK + 16
LINE = 8 * BLOCK + 16
DEPTH = 64
UNROLL = 4
SEGMENTS = 16
SEG_SLOTS = 2 * BLOCK + UNROLL
PACKED = 2 * BLOCK + SEGMENTS * (UNROLL - 1)
DST_ROWS = DST_BLK * BLOCK
HALF = DST_ROWS // 2
MIB = 1024 * 1024


def device(x, y, z, r):
    return (((x % NX) * NY + (y % NY)) * NZ + (z % NZ)) * 2 + r


def from_z(step):
    return [
        (device(x, y, 4 * r + (z + step) % 4, z // 4), device(x, y, z, r))
        for x in range(NX) for y in range(NY) for z in range(NZ) for r in range(2)
        if step or r != z // 4
    ]


def from_beside(step):
    return [
        (device(x, y, z - step if r else z + step, r), device(x, y, z, r))
        for x in range(NX) for y in range(NY) for z in range(NZ) for r in range(2)
    ]


def from_second(step):
    return [
        (device(x, y + step, z, 0) if r == 0 else device(x + step, y, z, 1), device(x, y, z, r))
        for x in range(NX) for y in range(NY) for z in range(NZ) for r in range(2)
    ]


def from_third(step):
    return [
        (device(x + step, y, z, 0) if r == 0 else device(x, y + step, z, 1), device(x, y, z, r))
        for x in range(NX) for y in range(NY) for z in range(NZ) for r in range(2)
    ]


def move(value, pairs):
    return lax.ppermute(value, ("col", "rep"), pairs)


def line_kernel(keep, own, c, d, b, a, swapped, slots, line):
    cut = 2 * BLOCK
    norms = []
    for k, shard in enumerate((a, b, c, d)):
        rows, norm = shard[pl.ds(0, cut), :], shard[pl.ds(cut, 16), :]
        if k == 0:
            rows = jnp.where(keep[0] != 0, own[pl.ds(0, cut), :], rows)
            norm = jnp.where(keep[0] != 0, own[pl.ds(cut, 16), :], norm)
        line[pl.ds(k * cut, cut), :] = rows
        norms.append(norm[:1].astype(jnp.float32))
    rows = jnp.concatenate(norms + [jnp.zeros((12, WIDTH), jnp.float32)], axis=0)
    line[pl.ds(8 * BLOCK, 16), :] = rows.astype(jnp.bfloat16)


def make_line(keep, shards, own, slots):
    vmem = pl.BlockSpec(memory_space=pltpu.VMEM)
    return pl.pallas_call(
        line_kernel,
        out_shape=jax.ShapeDtypeStruct((LINE, WIDTH), jnp.bfloat16),
        in_specs=[pl.BlockSpec(memory_space=pltpu.SMEM)] + [vmem] * 5
        + [pl.BlockSpec(memory_space=pltpu.HBM), pl.BlockSpec(memory_space=pl.ANY)],
        out_specs=vmem,
        compiler_params=pltpu.CompilerParams(vmem_limit_bytes=4 * MIB),
    )(keep, *shards, own, slots)


def sort_kernel(codes, base, slots, count, listed):
    def clear(k, carry):
        count[k] = 0
        return carry

    lax.fori_loop(0, SEGMENTS, clear, 0)

    def put(i, carry):
        for u in range(4):
            code = codes[4 * i + u]
            segment = (code >> 26) & 15
            at = count[segment]
            listed[segment * SEG_SLOTS + at] = code
            count[segment] = at + (code >> 30)
        return carry

    lax.fori_loop(0, 64, put, 0)

    def squeeze(k, at):
        base[k] = at
        size = count[k]
        for u in range(UNROLL - 1):
            listed[k * SEG_SLOTS + size + u] = 4 << 21
        groups = (size + (UNROLL - 1)) >> 2

        def copy(g, carry):
            for u in range(UNROLL):
                slots[(at + g) * UNROLL + u] = listed[k * SEG_SLOTS + g * UNROLL + u]
            return carry

        lax.fori_loop(0, groups, copy, 0)
        return at + groups

    base[SEGMENTS] = lax.fori_loop(0, SEGMENTS, squeeze, 0)


def sort_codes(codes):
    smem = pl.BlockSpec(memory_space=pltpu.SMEM)
    return pl.pallas_call(
        sort_kernel,
        out_shape=(
            jax.ShapeDtypeStruct((SEGMENTS + 1,), jnp.int32),
            jax.ShapeDtypeStruct((PACKED,), jnp.int32),
        ),
        in_specs=[smem],
        out_specs=(smem, smem),
        scratch_shapes=[
            pltpu.SMEM((SEGMENTS,), jnp.int32),
            pltpu.SMEM((SEGMENTS * SEG_SLOTS,), jnp.int32),
        ],
        compiler_params=pltpu.CompilerParams(vmem_limit_bytes=2 * MIB),
    )(codes)


def pack_kernel(base, slots, own, other, packed, tile, in_sem):
    total = base[SEGMENTS]

    def fetch(g):
        slot = lax.rem(g, DEPTH // UNROLL)
        for u in range(UNROLL):
            e = slots[g * UNROLL + u] & 255

            @pl.when(e < BLOCK)
            def _():
                pltpu.make_async_copy(own.at[e], tile.at[slot, u], in_sem.at[slot]).start()

            @pl.when(e >= BLOCK)
            def _():
                pltpu.make_async_copy(other.at[e - BLOCK], tile.at[slot, u], in_sem.at[slot]).start()

    def begin(g, carry):
        fetch(g)
        return carry

    ahead = DEPTH // UNROLL - 1
    lax.fori_loop(0, jnp.minimum(total, ahead), begin, 0)

    def step(g, carry):
        slot = lax.rem(g, DEPTH // UNROLL)

        @pl.when(g + ahead < total)
        def _():
            fetch(g + ahead)

        pltpu.make_async_copy(own.at[pl.ds(0, UNROLL)], tile.at[slot], in_sem.at[slot]).wait()

        packed[g] = tile[slot].astype(jnp.float32).astype(jnp.bfloat16)
        return carry

    lax.fori_loop(0, total, step, 0)


def pack_tiles(lists, own, other):
    smem = pl.BlockSpec(memory_space=pltpu.SMEM)
    hbm = pl.BlockSpec(memory_space=pltpu.HBM)
    ring = (DEPTH // UNROLL, UNROLL, BLOCK, BLOCK)
    return pl.pallas_call(
        pack_kernel,
        out_shape=jax.ShapeDtypeStruct((PACKED // UNROLL, UNROLL, BLOCK, BLOCK), jnp.bfloat16),
        in_specs=[smem, smem, hbm, hbm],
        out_specs=pl.BlockSpec(memory_space=pltpu.VMEM),
        scratch_shapes=[pltpu.VMEM(ring, jnp.int32), pltpu.SemaphoreType.DMA(ring[:1])],
        compiler_params=pltpu.CompilerParams(vmem_limit_bytes=20 * MIB),
        cost_estimate=pl.CostEstimate(flops=10**6, bytes_accessed=20 * 10**6, transcendentals=0),
    )(*lists, own, other)


def join_kernel(odd, c, a, b, d, packed, single, double):
    double[pl.ds(0, LINE), :] = b[...]
    double[pl.ds(LINE, LINE), :] = c[...]

    @pl.when(odd[0] == 0)
    def _():
        single[...] = a[...]

    @pl.when(odd[0] != 0)
    def _():
        single[...] = d[...]


def join_lines(odd, lines, packed):
    vmem = pl.BlockSpec(memory_space=pltpu.VMEM)
    return pl.pallas_call(
        join_kernel,
        out_shape=tuple(jax.ShapeDtypeStruct((n * LINE, WIDTH), jnp.bfloat16) for n in (1, 2)),
        in_specs=[pl.BlockSpec(memory_space=pltpu.SMEM)] + [vmem] * 4 + [pl.BlockSpec(memory_space=pl.ANY)],
        out_specs=(vmem, vmem),
        compiler_params=pltpu.CompilerParams(vmem_limit_bytes=8 * MIB),
    )(odd, lines[2], lines[0], lines[1], lines[3], packed)


def sum_kernel(ids, before, *refs):
    base, slots, packed = refs[:3]
    pieces = refs[3 : 3 + len(ids)]
    refs = refs[3 + len(ids) :]
    if before:
        earlier, refs = refs[0], refs[1:]
    if len(refs) > 2:
        sent, kept, norm, total = refs
    else:
        total, norm = refs
    if before:
        total[...] = earlier[...]
    else:
        total[...] = jnp.zeros_like(total)
    for i, piece in enumerate(pieces):
        for line in range(piece.shape[0] // LINE):
            for half in range(2):
                rows = piece[pl.ds(line * LINE + 8 * BLOCK, 16), pl.ds(half * BLOCK, BLOCK)]
                norm[pl.ds(32 * i + 16 * half + 8 * line, 8), :] = rows.astype(jnp.float32)[:8]
    for i, (k, piece) in enumerate(zip(ids, pieces)):
        first, last = base[k], base[k + 1]

        def add(g, groups, i=i, piece=piece):
            found = []
            for u in range(UNROLL * groups):
                code = slots[UNROLL * g + u]
                scale = norm[pl.ds(32 * i + ((code >> 21) & 31), 1), :]
                row = pl.multiple_of(((code >> 13) & 255) * 16, 16)
                found.append((
                    pl.multiple_of(((code >> 8) & 31) * BLOCK, BLOCK),
                    jnp.dot(
                        packed[g + u // UNROLL, u % UNROLL] * scale.astype(jnp.bfloat16),
                        piece[pl.ds(row, BLOCK), :], preferred_element_type=jnp.float32,
                    ),
                ))
            for at, product in found:
                total[pl.ds(at, BLOCK), :] += product

        def pair(j, carry, first=first, add=add):
            add(first + 2 * j, 2)
            return carry

        lax.fori_loop(0, (last - first) >> 1, pair, 0)

        @pl.when(((last - first) & 1) == 1)
        def _(last=last, add=add):
            add(last - 1, 1)

    if len(refs) > 2:
        sent[...] = total[pl.ds(0, HALF), :].astype(sent.dtype)
        kept[...] = total[pl.ds(HALF, HALF), :]


def sum_tiles(lists, pieces, earlier=None, last=False):
    smem = pl.BlockSpec(memory_space=pltpu.SMEM)
    vmem = pl.BlockSpec(memory_space=pltpu.VMEM)
    ids = tuple(pieces)
    before = [] if earlier is None else [earlier]
    whole = jax.ShapeDtypeStruct((DST_ROWS, WIDTH), jnp.float32)
    ends = tuple(jax.ShapeDtypeStruct((HALF, WIDTH), t) for t in (jnp.bfloat16, jnp.float32))
    norm = pltpu.VMEM((32 * len(ids), BLOCK), jnp.float32)
    return pl.pallas_call(
        functools.partial(sum_kernel, ids, bool(before)),
        out_shape=ends if last else whole,
        in_specs=[smem] * 2 + [vmem] * (1 + len(ids) + len(before)),
        out_specs=(vmem, vmem) if last else vmem,
        scratch_shapes=[norm] + ([pltpu.VMEM(whole.shape, whole.dtype)] if last else []),
        compiler_params=pltpu.CompilerParams(vmem_limit_bytes=8 * MIB),
        cost_estimate=pl.CostEstimate(flops=4 * 10**8, bytes_accessed=8 * 10**6, transcendentals=0),
    )(*lists, *pieces.values(), *before)


def finish_kernel(kept, received, scale, weight, bias, out, buffer, sems):
    step = HALF // 8
    copies = []
    for i in range(8):
        rows = pl.ds(i * step, step)
        tiles = [
            jnp.broadcast_to(scale[pl.ds(i * step // BLOCK + k, 1), :], (BLOCK, BLOCK)).T
            for k in range(step // BLOCK)
        ]
        factor = jnp.concatenate([jnp.concatenate(tiles, axis=0)] * 2, axis=1)
        aggregate = (kept[rows, :] + received[rows, :].astype(jnp.float32)) * factor
        result = jnp.dot(
            aggregate.astype(jnp.bfloat16), weight[...], preferred_element_type=jnp.float32
        ) + bias[...]
        buffer[rows, :] = jnp.maximum(result, 0.0).astype(jnp.bfloat16)
        copies.append(pltpu.make_async_copy(buffer.at[rows], out.at[rows], sems.at[i]))
        copies[-1].start()
    for copy in copies:
        copy.wait()


def finish(kept, received, scale, weight, bias):
    vmem = pl.BlockSpec(memory_space=pltpu.VMEM)
    return pl.pallas_call(
        finish_kernel,
        out_shape=jax.ShapeDtypeStruct((HALF, WIDTH), jnp.bfloat16),
        in_specs=[vmem] * 5,
        out_specs=pl.BlockSpec(memory_space=pl.ANY),
        scratch_shapes=[pltpu.VMEM((HALF, WIDTH), jnp.bfloat16), pltpu.SemaphoreType.DMA((8,))],
        compiler_params=pltpu.CompilerParams(vmem_limit_bytes=12 * MIB),
        cost_estimate=pl.CostEstimate(flops=3 * 10**8, bytes_accessed=6 * 10**6, transcendentals=0),
    )(kept, received, scale, weight, bias)


OWN_0, OWN_12, OWN_3 = 0, 1, 2
UP, UP_12, UP_Z = 4, 5, 6
FAR, FAR_12, FAR_Z = 8, 9, 10
DOWN, DOWN_12, DOWN_Z = 12, 13, 14


def encode(src, dst, place):
    z, second, third, rep = place
    entry = jnp.arange(2 * BLOCK, dtype=jnp.int32)
    p = src >> 1
    px, py, pz = p >> 5, (p >> 3) & 3, p & 7
    pa = jnp.where(rep == 0, py, px)
    pb = jnp.where(rep == 0, px, py)
    da, db = (pa - second) & 3, (pb - third) & 3
    double = (da == 1) | (da == 2)
    beside = (db != 0) & (da == jnp.where((z & 1) == 0, 3, 0))
    own_kind = jnp.where(double, 1, jnp.where(da == 0, 0, 2))
    far_kind = jnp.where(double, 1, jnp.where(beside, 2, 0))
    segment = db * 4 + jnp.where(db == 0, own_kind, far_kind)
    line = jnp.where(da == 2, 1, 0)
    z_of = jnp.where(beside, jnp.where((rep == 0) == (db != 3), z + 1, z - 1), z)
    shard = (pz - z_of) & 3
    d = (dst + 16 * (1 - rep)) & 31
    row16 = line * (LINE // 16) + shard * 16 + (src & 1) * 8
    scale = (src & 1) * 16 + line * 8 + shard
    valid = jnp.where((pz >> 2) == rep, 1, 0)
    return entry | (d << 8) | (row16 << 13) | (scale << 21) | (segment << 26) | (valid << 30)


def gather_shards(features, src_norm):
    norm_rows = jnp.broadcast_to(src_norm, (16, WIDTH))
    shard = jnp.concatenate([features, norm_rows], axis=0)
    return [shard] + [move(shard, from_z(step)) for step in (2, 3, 1, 0)]


def body(features, src_norm, dst_norm, src_block, dst_block, counts, weight, out_bias):
    rep = lax.axis_index("rep")
    col = lax.axis_index("col")
    x, y, z = col // (NY * NZ), (col // NZ) % NY, col % NZ
    swap = [(0, 1), (1, 0)]
    own = counts.reshape(-1, BLOCK, BLOCK)
    other = lax.ppermute(own, "rep", swap)
    ids = jnp.concatenate([src_block.reshape(1, -1), dst_block.reshape(1, -1)], axis=0)
    all_ids = lax.all_gather(ids, "rep")
    both = jnp.concatenate([ids, jnp.where(rep == 0, all_ids[1], all_ids[0])], axis=1)
    place = (z, jnp.where(rep == 0, y, x), jnp.where(rep == 0, x, y), rep)
    base, slots = sort_codes(encode(both[0], both[1], place))
    line_0 = make_line(
        jnp.where(z // 4 == rep, 1, 0).astype(jnp.int32).reshape(1), gather_shards(features, src_norm), other, slots)
    lines = [line_0] + [move(line_0, from_second(step)) for step in (1, 2, 3)]
    lists = (base, slots, pack_tiles((base, slots), own, other))
    single, double = join_lines((z & 1).astype(jnp.int32).reshape(1), lines, lists[2])
    up = move(single, from_third(1))
    down_12 = move(double, from_third(-1))
    up_12 = move(double, from_third(1))
    down = move(single, from_third(-1))
    up_z = move(up, from_beside(1))
    down_z = move(down, from_beside(-1))
    far = move(up, from_third(1))
    far_12 = move(down_12, from_third(-1))
    far_z = move(up_z, from_third(1))
    total = sum_tiles(lists, {OWN_0: lines[0], OWN_12: double, OWN_3: lines[3]})
    near = {UP: up, UP_Z: up_z, DOWN_12: down_12, DOWN: down, UP_12: up_12, FAR: far}
    total = sum_tiles(lists, near, total)
    sent, kept = sum_tiles(lists, {FAR_12: far_12, FAR_Z: far_z, DOWN_Z: down_z}, total, True)
    received = lax.ppermute(sent, "rep", swap)
    own_norm = lax.dynamic_slice_in_dim(dst_norm, rep * HALF, HALF, 0)
    scale = own_norm.reshape(HALF // BLOCK, BLOCK)
    return finish(kept, received, scale, weight, out_bias.astype(jnp.float32).reshape(1, -1))


def solution(mesh):
    placed = (
        P("col", None),
        P("col"),
        P("col"),
        P("col", "rep", None),
        P("col", "rep", None),
        P("col", "rep", None, None, None),
        P(),
        P(),
    )
    return jax.shard_map(
        body, mesh=mesh, in_specs=placed, out_specs=P(("col", "rep"), None), check_vma=False
    )
```

```python
import functools

import jax
import jax.numpy as jnp
from jax import lax
from jax.experimental import pallas as pl
from jax.experimental.pallas import tpu as pltpu
from jax.sharding import PartitionSpec as P

BLOCK = 128
DST_BLK = 32
WIDTH = 256
NX, NY, NZ = 4, 4, 8
SHARD = 2 * BLOCK + 16
LINE = 8 * BLOCK + 16
DEPTH = 64
UNROLL = 4
SEGMENTS = 16
SEG_SLOTS = 2 * BLOCK + UNROLL
PACKED = 2 * BLOCK + SEGMENTS * (UNROLL - 1)
DST_ROWS = DST_BLK * BLOCK
HALF = DST_ROWS // 2
MIB = 1024 * 1024


def device(x, y, z, r):
    return (((x % NX) * NY + (y % NY)) * NZ + (z % NZ)) * 2 + r


def from_z(step):
    return [
        (device(x, y, 4 * r + (z + step) % 4, z // 4), device(x, y, z, r))
        for x in range(NX) for y in range(NY) for z in range(NZ) for r in range(2)
        if step or r != z // 4
    ]


def from_beside(step):
    return [
        (device(x, y, z - step if r else z + step, r), device(x, y, z, r))
        for x in range(NX) for y in range(NY) for z in range(NZ) for r in range(2)
    ]


def from_second(step):
    return [
        (device(x, y + step, z, 0) if r == 0 else device(x + step, y, z, 1), device(x, y, z, r))
        for x in range(NX) for y in range(NY) for z in range(NZ) for r in range(2)
    ]


def from_third(step):
    return [
        (device(x + step, y, z, 0) if r == 0 else device(x, y + step, z, 1), device(x, y, z, r))
        for x in range(NX) for y in range(NY) for z in range(NZ) for r in range(2)
    ]


def move(value, pairs):
    return lax.ppermute(value, ("col", "rep"), pairs)


def line_kernel(keep, own, c, d, b, a, swapped, slots, line):
    cut = 2 * BLOCK
    norms = []
    for k, shard in enumerate((a, b, c, d)):
        rows, norm = shard[pl.ds(0, cut), :], shard[pl.ds(cut, 16), :]
        if k == 0:
            rows = jnp.where(keep[0] != 0, own[pl.ds(0, cut), :], rows)
            norm = jnp.where(keep[0] != 0, own[pl.ds(cut, 16), :], norm)
        line[pl.ds(k * cut, cut), :] = rows
        norms.append(norm[:1].astype(jnp.float32))
    rows = jnp.concatenate(norms + [jnp.zeros((12, WIDTH), jnp.float32)], axis=0)
    line[pl.ds(8 * BLOCK, 16), :] = rows.astype(jnp.bfloat16)


def make_line(keep, shards, own, slots):
    vmem = pl.BlockSpec(memory_space=pltpu.VMEM)
    return pl.pallas_call(
        line_kernel,
        out_shape=jax.ShapeDtypeStruct((LINE, WIDTH), jnp.bfloat16),
        in_specs=[pl.BlockSpec(memory_space=pltpu.SMEM)] + [vmem] * 5
        + [pl.BlockSpec(memory_space=pltpu.HBM), pl.BlockSpec(memory_space=pl.ANY)],
        out_specs=vmem,
        compiler_params=pltpu.CompilerParams(vmem_limit_bytes=4 * MIB),
    )(keep, *shards, own, slots)


def sort_kernel(codes, base, slots, count, listed):
    def clear(k, carry):
        count[k] = 0
        return carry

    lax.fori_loop(0, SEGMENTS, clear, 0)

    def put(i, carry):
        for u in range(4):
            code = codes[4 * i + u]
            segment = (code >> 26) & 15
            at = count[segment]
            listed[segment * SEG_SLOTS + at] = code
            count[segment] = at + (code >> 30)
        return carry

    lax.fori_loop(0, 64, put, 0)

    def squeeze(k, at):
        base[k] = at
        size = count[k]
        for u in range(UNROLL - 1):
            listed[k * SEG_SLOTS + size + u] = 4 << 21
        groups = (size + (UNROLL - 1)) >> 2

        def copy(g, carry):
            for u in range(UNROLL):
                slots[(at + g) * UNROLL + u] = listed[k * SEG_SLOTS + g * UNROLL + u]
            return carry

        lax.fori_loop(0, groups, copy, 0)
        return at + groups

    base[SEGMENTS] = lax.fori_loop(0, SEGMENTS, squeeze, 0)


def sort_codes(codes):
    smem = pl.BlockSpec(memory_space=pltpu.SMEM)
    return pl.pallas_call(
        sort_kernel,
        out_shape=(
            jax.ShapeDtypeStruct((SEGMENTS + 1,), jnp.int32),
            jax.ShapeDtypeStruct((PACKED,), jnp.int32),
        ),
        in_specs=[smem],
        out_specs=(smem, smem),
        scratch_shapes=[
            pltpu.SMEM((SEGMENTS,), jnp.int32),
            pltpu.SMEM((SEGMENTS * SEG_SLOTS,), jnp.int32),
        ],
        compiler_params=pltpu.CompilerParams(vmem_limit_bytes=2 * MIB),
    )(codes)


def pack_kernel(base, slots, own, other, packed, tile, in_sem):
    total = base[SEGMENTS]

    def fetch(g):
        slot = lax.rem(g, DEPTH // UNROLL)
        for u in range(UNROLL):
            e = slots[g * UNROLL + u] & 255

            @pl.when(e < BLOCK)
            def _():
                pltpu.make_async_copy(own.at[e], tile.at[slot, u], in_sem.at[slot]).start()

            @pl.when(e >= BLOCK)
            def _():
                pltpu.make_async_copy(other.at[e - BLOCK], tile.at[slot, u], in_sem.at[slot]).start()

    def begin(g, carry):
        fetch(g)
        return carry

    ahead = DEPTH // UNROLL - 1
    lax.fori_loop(0, jnp.minimum(total, ahead), begin, 0)

    def step(g, carry):
        slot = lax.rem(g, DEPTH // UNROLL)

        @pl.when(g + ahead < total)
        def _():
            fetch(g + ahead)

        pltpu.make_async_copy(own.at[pl.ds(0, UNROLL)], tile.at[slot], in_sem.at[slot]).wait()

        packed[g] = tile[slot].astype(jnp.float32).astype(jnp.bfloat16)
        return carry

    lax.fori_loop(0, total, step, 0)


def pack_tiles(lists, own, other):
    smem = pl.BlockSpec(memory_space=pltpu.SMEM)
    hbm = pl.BlockSpec(memory_space=pltpu.HBM)
    ring = (DEPTH // UNROLL, UNROLL, BLOCK, BLOCK)
    return pl.pallas_call(
        pack_kernel,
        out_shape=jax.ShapeDtypeStruct((PACKED // UNROLL, UNROLL, BLOCK, BLOCK), jnp.bfloat16),
        in_specs=[smem, smem, hbm, hbm],
        out_specs=pl.BlockSpec(memory_space=pltpu.VMEM),
        scratch_shapes=[pltpu.VMEM(ring, jnp.int32), pltpu.SemaphoreType.DMA(ring[:1])],
        compiler_params=pltpu.CompilerParams(vmem_limit_bytes=20 * MIB),
        cost_estimate=pl.CostEstimate(flops=10**6, bytes_accessed=20 * 10**6, transcendentals=0),
    )(*lists, own, other)


def join_kernel(odd, c, a, b, d, packed, single, double):
    double[pl.ds(0, LINE), :] = b[...]
    double[pl.ds(LINE, LINE), :] = c[...]

    @pl.when(odd[0] == 0)
    def _():
        single[...] = a[...]

    @pl.when(odd[0] != 0)
    def _():
        single[...] = d[...]


def join_lines(odd, lines, packed):
    vmem = pl.BlockSpec(memory_space=pltpu.VMEM)
    return pl.pallas_call(
        join_kernel,
        out_shape=tuple(jax.ShapeDtypeStruct((n * LINE, WIDTH), jnp.bfloat16) for n in (1, 2)),
        in_specs=[pl.BlockSpec(memory_space=pltpu.SMEM)] + [vmem] * 4 + [pl.BlockSpec(memory_space=pl.ANY)],
        out_specs=(vmem, vmem),
        compiler_params=pltpu.CompilerParams(vmem_limit_bytes=8 * MIB),
    )(odd, lines[2], lines[0], lines[1], lines[3], packed)


def sum_kernel(ids, before, last, *refs):
    base, slots, packed = refs[:3]
    pieces = refs[3 : 3 + len(ids)]
    refs = refs[3 + len(ids) :]
    if before:
        earlier, refs = refs[0], refs[1:]
    if last:
        sent, kept, norm, low = refs
        low[...] = earlier[pl.ds(0, HALF), :]
        kept[...] = earlier[pl.ds(HALF, HALF), :]
        parts = [(i, k, low, 0) for i, k in enumerate(ids)]
        parts += [(i, UPPER[k], kept, HALF) for i, k in enumerate(ids)]
    else:
        total, norm = refs
        if before:
            total[...] = earlier[...]
        else:
            total[...] = jnp.zeros_like(total)
        parts = [(i, k, total, 0) for i, k in enumerate(ids)]
    for i, piece in enumerate(pieces):
        for line in range(piece.shape[0] // LINE):
            for half in range(2):
                rows = piece[pl.ds(line * LINE + 8 * BLOCK, 16), pl.ds(half * BLOCK, BLOCK)]
                norm[pl.ds(32 * i + 16 * half + 8 * line, 8), :] = rows.astype(jnp.float32)[:8]
    for i, k, total, first_row in parts:
        first, end = base[k], base[k + 1]

        def add(g, groups, i=i, piece=pieces[i], total=total, first_row=first_row):
            found = []
            for u in range(UNROLL * groups):
                code = slots[UNROLL * g + u]
                scale = norm[pl.ds(32 * i + ((code >> 21) & 31), 1), :]
                row = pl.multiple_of(((code >> 13) & 255) * 16, 16)
                found.append((
                    pl.multiple_of(jnp.maximum(((code >> 8) & 31) * BLOCK - first_row, 0), BLOCK),
                    jnp.dot(
                        packed[g + u // UNROLL, u % UNROLL] * scale.astype(jnp.bfloat16),
                        piece[pl.ds(row, BLOCK), :], preferred_element_type=jnp.float32,
                    ),
                ))
            for at, product in found:
                total[pl.ds(at, BLOCK), :] += product

        def pair(j, carry, first=first, add=add):
            add(first + 2 * j, 2)
            return carry

        lax.fori_loop(0, (end - first) >> 1, pair, 0)

        @pl.when(((end - first) & 1) == 1)
        def _(end=end, add=add):
            add(end - 1, 1)

    if last:
        sent[...] = low[...].astype(sent.dtype)


def sum_tiles(lists, pieces, earlier=None, last=False):
    smem = pl.BlockSpec(memory_space=pltpu.SMEM)
    vmem = pl.BlockSpec(memory_space=pltpu.VMEM)
    ids = tuple(pieces)
    before = [] if earlier is None else [earlier]
    whole = jax.ShapeDtypeStruct((DST_ROWS, WIDTH), jnp.float32)
    ends = tuple(jax.ShapeDtypeStruct((HALF, WIDTH), t) for t in (jnp.bfloat16, jnp.float32))
    norm = pltpu.VMEM((32 * len(ids), BLOCK), jnp.float32)
    return pl.pallas_call(
        functools.partial(sum_kernel, ids, bool(before), last),
        out_shape=ends if last else whole,
        in_specs=[smem] * 2 + [vmem] * (1 + len(ids) + len(before)),
        out_specs=(vmem, vmem) if last else vmem,
        scratch_shapes=[norm] + ([pltpu.VMEM((HALF, WIDTH), jnp.float32)] if last else []),
        compiler_params=pltpu.CompilerParams(vmem_limit_bytes=8 * MIB),
        cost_estimate=pl.CostEstimate(flops=4 * 10**8, bytes_accessed=8 * 10**6, transcendentals=0),
    )(*lists, *pieces.values(), *before)


def finish_kernel(kept, received, scale, weight, bias, out, buffer, sems):
    step = HALF // 8
    copies = []
    for i in range(8):
        rows = pl.ds(i * step, step)
        tiles = [
            jnp.broadcast_to(scale[pl.ds(i * step // BLOCK + k, 1), :], (BLOCK, BLOCK)).T
            for k in range(step // BLOCK)
        ]
        factor = jnp.concatenate([jnp.concatenate(tiles, axis=0)] * 2, axis=1)
        aggregate = (kept[rows, :] + received[rows, :].astype(jnp.float32)) * factor
        result = jnp.dot(
            aggregate.astype(jnp.bfloat16), weight[...], preferred_element_type=jnp.float32
        ) + bias[...]
        buffer[rows, :] = jnp.maximum(result, 0.0).astype(jnp.bfloat16)
        copies.append(pltpu.make_async_copy(buffer.at[rows], out.at[rows], sems.at[i]))
        copies[-1].start()
    for copy in copies:
        copy.wait()


def finish(kept, received, scale, weight, bias):
    vmem = pl.BlockSpec(memory_space=pltpu.VMEM)
    return pl.pallas_call(
        finish_kernel,
        out_shape=jax.ShapeDtypeStruct((HALF, WIDTH), jnp.bfloat16),
        in_specs=[vmem] * 5,
        out_specs=pl.BlockSpec(memory_space=pl.ANY),
        scratch_shapes=[pltpu.VMEM((HALF, WIDTH), jnp.bfloat16), pltpu.SemaphoreType.DMA((8,))],
        compiler_params=pltpu.CompilerParams(vmem_limit_bytes=12 * MIB),
        cost_estimate=pl.CostEstimate(flops=3 * 10**8, bytes_accessed=6 * 10**6, transcendentals=0),
    )(kept, received, scale, weight, bias)


OWN_0, OWN_12, OWN_3 = 0, 1, 2
UP, UP_12, UP_Z = 4, 5, 6
FAR, FAR_12, FAR_Z = 8, 9, 10
DOWN, DOWN_12, DOWN_Z = 12, 13, 14
UPPER = {FAR_12: 3, FAR_Z: 7, DOWN_Z: 11}


def encode(src, dst, place):
    z, second, third, rep = place
    entry = jnp.arange(2 * BLOCK, dtype=jnp.int32)
    p = src >> 1
    px, py, pz = p >> 5, (p >> 3) & 3, p & 7
    pa = jnp.where(rep == 0, py, px)
    pb = jnp.where(rep == 0, px, py)
    da, db = (pa - second) & 3, (pb - third) & 3
    double = (da == 1) | (da == 2)
    beside = (db != 0) & (da == jnp.where((z & 1) == 0, 3, 0))
    own_kind = jnp.where(double, 1, jnp.where(da == 0, 0, 2))
    far_kind = jnp.where(double, 1, jnp.where(beside, 2, 0))
    segment = db * 4 + jnp.where(db == 0, own_kind, far_kind)
    d = (dst + 16 * (1 - rep)) & 31
    for low, high in UPPER.items():
        segment = jnp.where((segment == low) & (d >= 16), high, segment)
    line = jnp.where(da == 2, 1, 0)
    z_of = jnp.where(beside, jnp.where((rep == 0) == (db != 3), z + 1, z - 1), z)
    shard = (pz - z_of) & 3
    d = (dst + 16 * (1 - rep)) & 31
    row16 = line * (LINE // 16) + shard * 16 + (src & 1) * 8
    scale = (src & 1) * 16 + line * 8 + shard
    valid = jnp.where((pz >> 2) == rep, 1, 0)
    return entry | (d << 8) | (row16 << 13) | (scale << 21) | (segment << 26) | (valid << 30)


def gather_shards(features, src_norm):
    norm_rows = jnp.broadcast_to(src_norm, (16, WIDTH))
    shard = jnp.concatenate([features, norm_rows], axis=0)
    return [shard] + [move(shard, from_z(step)) for step in (2, 3, 1, 0)]


def body(features, src_norm, dst_norm, src_block, dst_block, counts, weight, out_bias):
    rep = lax.axis_index("rep")
    col = lax.axis_index("col")
    x, y, z = col // (NY * NZ), (col // NZ) % NY, col % NZ
    swap = [(0, 1), (1, 0)]
    own = counts.reshape(-1, BLOCK, BLOCK)
    other = lax.ppermute(own, "rep", swap)
    ids = jnp.concatenate([src_block.reshape(1, -1), dst_block.reshape(1, -1)], axis=0)
    all_ids = lax.all_gather(ids, "rep")
    both = jnp.concatenate([ids, jnp.where(rep == 0, all_ids[1], all_ids[0])], axis=1)
    place = (z, jnp.where(rep == 0, y, x), jnp.where(rep == 0, x, y), rep)
    base, slots = sort_codes(encode(both[0], both[1], place))
    line_0 = make_line(
        jnp.where(z // 4 == rep, 1, 0).astype(jnp.int32).reshape(1), gather_shards(features, src_norm), other, slots)
    lines = [line_0] + [move(line_0, from_second(step)) for step in (1, 2, 3)]
    lists = (base, slots, pack_tiles((base, slots), own, other))
    single, double = join_lines((z & 1).astype(jnp.int32).reshape(1), lines, lists[2])
    up = move(single, from_third(1))
    down_12 = move(double, from_third(-1))
    up_12 = move(double, from_third(1))
    down = move(single, from_third(-1))
    up_z = move(up, from_beside(1))
    down_z = move(down, from_beside(-1))
    far = move(up, from_third(1))
    far_12 = move(down_12, from_third(-1))
    far_z = move(up_z, from_third(1))
    total = sum_tiles(lists, {OWN_0: lines[0], OWN_12: double, OWN_3: lines[3]})
    near = {UP: up, UP_Z: up_z, DOWN_12: down_12, DOWN: down, UP_12: up_12, FAR: far}
    total = sum_tiles(lists, near, total)
    sent, kept = sum_tiles(lists, {FAR_12: far_12, FAR_Z: far_z, DOWN_Z: down_z}, total, True)
    received = lax.ppermute(sent, "rep", swap)
    own_norm = lax.dynamic_slice_in_dim(dst_norm, rep * HALF, HALF, 0)
    scale = own_norm.reshape(HALF // BLOCK, BLOCK)
    return finish(kept, received, scale, weight, out_bias.astype(jnp.float32).reshape(1, -1))


def solution(mesh):
    placed = (
        P("col", None),
        P("col"),
        P("col"),
        P("col", "rep", None),
        P("col", "rep", None),
        P("col", "rep", None, None, None),
        P(),
        P(),
    )
    return jax.shard_map(
        body, mesh=mesh, in_specs=placed, out_specs=P(("col", "rep"), None), check_vma=False
    )
```
